32 devices in a mesh: grp: 2 (over x), lon: 16 (over z, y, core).
Axes of the slice: x: 2, y: 2, z: 4, core: 2. Of those that a mesh axis runs over, the one named last changes fastest.
Arguments:
- features: bfloat16 [32, 16, 4096, 128], P(('grp', 'lon')), parts along dimension 0, may hold values from -6 to 6
- conv_weight: bfloat16 [3, 3, 128, 64], replicated, may hold values from -0.1875 to 0.1875
- conv_bias: float32 [64], replicated, may hold values from -3 to 3
- head_weight: bfloat16 [64, 4], replicated, may hold values from -0.75 to 0.75
- head_bias: float32 [4], replicated, may hold values from -3 to 3
Outputs:
- peak_margin: float32 [32, 16, 4096], P(('grp', 'lon')), parts along dimension 0
- regress: float32 [32, 3, 16, 4096], P(('grp', 'lon')), parts along dimension 0
The draws below stay inside these ranges and needn't reach their ends.
There are 2 independent parts, one for each index of `grp`. The reference program is written for one: setup_inputs(seed, part) draws one part's arguments, and reference() takes and returns one part's arrays. A program takes and returns all parts, laid end to end along the dimension named above; an argument that names none is the same for every part. Nothing has to cross between parts.
All inputs are finite; a program needn't handle non-finite values.
Results may differ from the reference program's by a relative error of at most 0.008.
Values may be sent and summed in bfloat16 or wider, within the bound.
A program may use at most 384 MiB of HBM per device.

```python
from functools import reduce
import jax
import jax.numpy as jnp

C = 128
HID = 64
LATT = 4
TILE_H = 16
TILE_W = 4096
TILES = 16


def block_scale(own_key, extent, cuts, low, high):
    level, own = 1.0, jax.random.fold_in(own_key, 6)
    for dim, blocks in cuts:
        steps = jnp.exp(jax.random.uniform(jax.random.fold_in(own, dim), (blocks,), jnp.float32, low / len(cuts), high / len(cuts)))
        level = level * jnp.repeat(steps, extent[dim] // blocks).reshape([-1 if axis == dim else 1 for axis in range(len(extent))])
    return level


def bell_draw(own_key, shape, width, bound, pieces=(), kind=jnp.bfloat16):
    array = width * jax.random.normal(own_key, shape, jnp.float32)
    if pieces:
        array = array * block_scale(own_key, shape, pieces, -0.22, 0.18)
    return jnp.clip(array, -bound, bound).astype(kind)


def setup_inputs(seed: int = 0, part: int = 0) -> dict:
    key_list = jax.random.split(jax.random.key(seed), 6)
    part_keys = jax.random.split(jax.random.fold_in(key_list[5], part), 6)
    return {
        "features": bell_draw(part_keys[0], (TILES, TILE_H, TILE_W, C), 1.0, 6.0, ((0, 16),)),
        "conv_weight": bell_draw(key_list[1], (3, 3, C, HID), (9 * C) ** -0.5, 0.1875),
        "conv_bias": bell_draw(key_list[2], (HID,), 0.5, 3.0, (), jnp.float32),
        "head_weight": bell_draw(key_list[3], (HID, 4), HID ** -0.5, 0.75),
        "head_bias": bell_draw(key_list[4], (4,), 1.0, 3.0, (), jnp.float32),
    }


def assemble(tile_stack):
    lon_tiles = tile_stack.shape[0] // LATT
    shaped = tile_stack.reshape((lon_tiles, LATT) + tile_stack.shape[1:])
    shaped = jnp.moveaxis(shaped, 0, 2)
    return shaped.reshape((LATT * tile_stack.shape[1], lon_tiles * tile_stack.shape[2]) + tile_stack.shape[3:])


def lat_partial(rows, weight_tap, col_count):
    row_total = rows.shape[0]
    chans = rows.shape[2]
    hid_count = weight_tap.shape[2]
    stacked = jnp.transpose(weight_tap, (1, 0, 2)).reshape(chans, 3 * hid_count)
    product = jnp.dot(rows.reshape(row_total * (col_count + 2), chans), stacked, preferred_element_type=jnp.float32)
    product = product.reshape(row_total, col_count + 2, 3, hid_count)
    summed = product[:, 0:col_count, 0] + product[:, 1:col_count + 1, 1]
    summed = summed + product[:, 2:col_count + 2, 2]
    return summed.astype(jnp.bfloat16)


def reference(features, conv_weight, conv_bias, head_weight, head_bias):
    band_cells = assemble(jnp.roll(features, 1, axis=0))
    row_count = band_cells.shape[0]
    col_count = band_cells.shape[1]
    wrapped = jnp.concatenate([band_cells[:, col_count - 1:], band_cells, band_cells[:, :1]], axis=1)
    padded = jnp.pad(wrapped, ((1, 1), (0, 0), (0, 0)))
    hidden_blocks = []
    for block in range(LATT):
        start = block * TILE_H
        pre_act = conv_bias.astype(jnp.float32)
        for tap in range(3):
            rows = padded[start + tap:start + tap + TILE_H]
            pre_act = pre_act + lat_partial(rows, conv_weight[tap], col_count).astype(jnp.float32)
        hidden_blocks.append(jax.nn.relu(pre_act).astype(jnp.bfloat16))
    hidden = jnp.concatenate(hidden_blocks, axis=0)
    logits = jnp.einsum("kj,hwk->jhw", head_weight.astype(jnp.float32), hidden.astype(jnp.float32))
    logits = logits + head_bias[:, None, None]
    heatmap = jax.nn.sigmoid(logits[0])
    heat_wrap = jnp.concatenate([heatmap[:, col_count - 4:], heatmap, heatmap[:, :4]], axis=1)
    heat_pad = jnp.pad(heat_wrap, ((4, 4), (0, 0)))
    full_max = reduce(jnp.maximum, [heat_pad[:, sx:sx + col_count] for sx in range(9)])
    side_max = reduce(jnp.maximum, [heat_pad[4:4 + row_count, sx:sx + col_count] for sx in range(9) if sx != 4])
    others = reduce(jnp.maximum, [full_max[sy:sy + row_count] for sy in range(9) if sy != 4])
    margin_full = heat_pad[4:4 + row_count, 4:4 + col_count] - jnp.maximum(others, side_max)
    lon_tiles = col_count // TILE_W
    peak_margin = margin_full.reshape(LATT, TILE_H, lon_tiles, TILE_W).transpose(2, 0, 1, 3).reshape(lon_tiles * LATT, TILE_H, TILE_W)
    regress = logits[1:].reshape(3, LATT, TILE_H, lon_tiles, TILE_W).transpose(3, 1, 0, 2, 4).reshape(lon_tiles * LATT, 3, TILE_H, TILE_W)
    return jnp.roll(peak_margin, -1, axis=0), jnp.roll(regress, -1, axis=0)
```

```python
import jax
import jax.numpy as jnp
from jax import lax
from jax.experimental import pallas as pl
from jax.experimental.pallas import tpu as pltpu
from jax.sharding import PartitionSpec as P

LATT = 4
CB = 512
PAD = 16
LANES = 128
MESH = pl.DeviceIdType.MESH


def kernel(
    n, x_ref, cw_ref, cb_ref, hw_ref, hb_ref, margin_ref, regress_ref,
    xbuf, wbuf, hbig, pre_edge, hid, lg, sendbuf, recvbuf, hs,
    x_sem, rim_send, rim_recv, lat_send, lat_recv, heat_send, heat_recv,
):
    rows, cols = xbuf.shape[0], xbuf.shape[1] - 2 * PAD
    pairs = rows // 2
    blocks = cols // CB
    half = CB // 2
    t = lax.axis_index("lon")
    lat = lax.rem(t + 1, LATT)
    has_north = lat != 0
    has_south = lat != LATT - 1
    grp = lax.axis_index("grp")

    def dev(shift):
        return (grp, lax.rem(t + shift + n, n))

    north, south, west, east = dev(-1), dev(1), dev(-LATT), dev(LATT)

    def own_copy(c):
        start = pl.multiple_of(c * CB, CB)
        return pltpu.make_async_copy(
            x_ref.at[0, :, pl.ds(start, CB)],
            xbuf.at[:, pl.ds(PAD + start, CB)],
            x_sem.at[c],
        )

    for c in range(blocks):
        own_copy(c).start()

    barrier = pltpu.get_barrier_semaphore()

    def greet(target):
        pl.semaphore_signal(barrier, inc=1, device_id=target, device_id_type=MESH)

    greet(west)
    greet(east)

    @pl.when(has_north)
    def _():
        greet(north)
        greet(dev(-1 - LATT))
        greet(dev(-1 + LATT))

    @pl.when(has_south)
    def _():
        greet(south)
        greet(dev(1 - LATT))
        greet(dev(1 + LATT))

    zero_tap = jnp.zeros((LANES, 64), jnp.bfloat16)

    def tap(a, b):
        return cw_ref[a, b] if 0 <= a <= 2 else zero_tap

    for b in range(3):
        for s in range(2):
            lo = (b * 2 + s) * LANES
            wbuf[lo : lo + LANES, 0:LANES] = jnp.concatenate([tap(s + 1, b), tap(s, b)], axis=1)
            wbuf[lo : lo + LANES, LANES : 2 * LANES] = jnp.concatenate(
                [tap(s - 1, b), tap(s + 2, b)], axis=1
            )
    spread = (
        lax.broadcasted_iota(jnp.int32, (4 * rows, 4), 0) // rows
        == lax.broadcasted_iota(jnp.int32, (4 * rows, 4), 1)
    )
    spread = jnp.where(spread, 1.0, 0.0).astype(jnp.bfloat16)
    by_row = lax.dot_general(
        spread, hw_ref[...], (((1,), (1,)), ((), ())), preferred_element_type=jnp.float32
    )
    wide = jnp.concatenate([by_row] * rows, axis=1)
    keep = (
        lax.rem(lax.broadcasted_iota(jnp.int32, wide.shape, 0), rows)
        == lax.broadcasted_iota(jnp.int32, wide.shape, 1) // 64
    )
    hbig[...] = jnp.where(keep, wide, 0.0).astype(jnp.bfloat16)

    @pl.when(jnp.logical_not(has_north))
    def _():
        recvbuf[0] = jnp.zeros(recvbuf.shape[1:], recvbuf.dtype)
        hs[0:8, :] = jnp.zeros((8, hs.shape[1]), hs.dtype)

    @pl.when(jnp.logical_not(has_south))
    def _():
        recvbuf[1] = jnp.zeros(recvbuf.shape[1:], recvbuf.dtype)
        hs[8 + rows : 16 + rows, :] = jnp.zeros((8, hs.shape[1]), hs.dtype)

    peers = 2 + jnp.where(has_north, 3, 0) + jnp.where(has_south, 3, 0)
    pl.semaphore_wait(barrier, peers)

    def remote(src, dst, send, recv, target):
        return pltpu.make_async_remote_copy(
            src_ref=src, dst_ref=dst, send_sem=send, recv_sem=recv,
            device_id=target, device_id_type=MESH,
        )

    to_east = remote(
        x_ref.at[0, :, pl.ds(cols - PAD, PAD)], xbuf.at[:, pl.ds(0, PAD)],
        rim_send.at[0], rim_recv.at[0], east,
    )
    to_west = remote(
        x_ref.at[0, :, pl.ds(0, PAD)], xbuf.at[:, pl.ds(cols + PAD, PAD)],
        rim_send.at[1], rim_recv.at[1], west,
    )
    to_east.start()
    to_west.start()

    low_lane = lax.broadcasted_iota(jnp.int32, (1, LANES), 1) < 64
    bias = jnp.concatenate([cb_ref[...], cb_ref[...]], axis=1)

    def lat_copy(way, c):
        part = pl.ds(pl.multiple_of(c * half, half), half)
        return remote(
            sendbuf.at[way, part], recvbuf.at[way, part],
            lat_send.at[way, c], lat_recv.at[way, c], south if way == 0 else north,
        )

    own_copy(0).wait()
    own_copy(1).wait()

    def first(i, carry):
        c = lax.rem(i + 1, blocks)
        base = pl.multiple_of(c * CB, CB)

        @pl.when(i + 2 < blocks)
        def _():
            own_copy(i + 2).wait()

        @pl.when(i == blocks - 2)
        def _():
            to_west.wait_recv()

        @pl.when(i == blocks - 1)
        def _():
            to_east.wait_recv()

        def products(p):
            win = jnp.concatenate(
                [xbuf[2 * p, pl.ds(base, CB + 2 * PAD)], xbuf[2 * p + 1, pl.ds(base, CB + 2 * PAD)]],
                axis=1,
            )
            taps = jnp.concatenate(
                [win[PAD - 1 + b : PAD - 1 + b + CB] for b in range(3)], axis=1
            )
            return jnp.dot(taps, wbuf[...], preferred_element_type=jnp.float32)

        def finish(p, main, above, below):
            pre = main + bias
            if p == 0:
                pre_edge[0, pl.ds(base, CB)] = pre + jnp.where(low_lane, 0.0, below)
            elif p == pairs - 1:
                pre_edge[1, pl.ds(base, CB)] = pre + jnp.where(low_lane, above, 0.0)
            else:
                pre = pre + jnp.where(low_lane, above, below)
                at = (p - 1) * LANES
                hid[:, at : at + LANES] = jnp.maximum(pre, 0.0).astype(jnp.bfloat16)

        before = None
        held = None
        for p in range(pairs):
            out = products(p)
            main, side = out[:, :LANES], out[:, LANES:]
            if p == 0:
                packed = jnp.where(low_lane, pltpu.roll(side[:half], 64, 1), side[half:])
                sendbuf[1, pl.ds(pl.multiple_of(c * half, half), half)] = packed.astype(jnp.bfloat16)
            else:
                finish(p - 1, held[0], before, side)
                before = held[1]
            held = (main, side)
        packed = jnp.where(low_lane, held[1][:half], pltpu.roll(held[1][half:], 64, 1))
        sendbuf[0, pl.ds(pl.multiple_of(c * half, half), half)] = packed.astype(jnp.bfloat16)
        finish(pairs - 1, held[0], before, None)

        @pl.when(has_south)
        def _():
            lat_copy(0, c).start()

        @pl.when(has_north)
        def _():
            lat_copy(1, c).start()

        lg[:, pl.ds(base, CB)] = lax.dot_general(
            hbig[:, LANES : (pairs - 1) * LANES], hid[...],
            (((1,), (1,)), ((), ())), preferred_element_type=jnp.float32,
        )
        return carry

    lax.fori_loop(0, blocks, first, 0)

    def second(i, carry):
        c = lax.rem(i + 1, blocks)
        base = pl.multiple_of(c * CB, CB)
        part = pl.ds(pl.multiple_of(c * half, half), half)

        @pl.when(has_north)
        def _():
            lat_copy(0, c).wait_recv()

        @pl.when(has_south)
        def _():
            lat_copy(1, c).wait_recv()

        above = recvbuf[0, part].astype(jnp.float32)
        above = jnp.concatenate([above, pltpu.roll(above, 64, 1)], axis=0)
        below = recvbuf[1, part].astype(jnp.float32)
        below = jnp.concatenate([pltpu.roll(below, 64, 1), below], axis=0)
        top = pre_edge[0, pl.ds(base, CB)] + jnp.where(low_lane, above, 0.0)
        bottom = pre_edge[1, pl.ds(base, CB)] + jnp.where(low_lane, 0.0, below)
        edge = jnp.maximum(jnp.concatenate([top, bottom], axis=1), 0.0).astype(jnp.bfloat16)
        heads = jnp.concatenate([hbig[:, :LANES], hbig[:, (pairs - 1) * LANES :]], axis=1)
        logits = lg[:, pl.ds(base, CB)] + lax.dot_general(
            heads, edge, (((1,), (1,)), ((), ())), preferred_element_type=jnp.float32
        )
        hs[8 : 8 + rows, pl.ds(LANES + base, CB)] = jax.nn.sigmoid(logits[:rows] + hb_ref[0])
        for k in range(1, 4):
            regress_ref[0, k - 1, :, pl.ds(base, CB)] = (
                logits[k * rows : (k + 1) * rows] + hb_ref[k]
            )
        return carry

    lax.fori_loop(0, blocks, second, 0)

    own, far = pl.ds(8, rows), pl.ds(LANES + cols, LANES)
    first_cols, last_cols = pl.ds(LANES, LANES), pl.ds(cols, LANES)
    near = pl.ds(0, LANES)
    mid = pl.ds(LANES, cols)
    first_rows, last_rows = pl.ds(8, 8), pl.ds(rows, 8)
    over, under = pl.ds(0, 8), pl.ds(8 + rows, 8)

    def heat(k, src, dst, target):
        return remote(hs.at[src], hs.at[dst], heat_send.at[k], heat_recv.at[k], target)

    lon_heat = [
        heat(0, (own, last_cols), (own, near), east),
        heat(1, (own, first_cols), (own, far), west),
    ]
    down_heat = [
        heat(2, (last_rows, mid), (over, mid), south),
        heat(3, (last_rows, last_cols), (over, near), dev(1 + LATT)),
        heat(4, (last_rows, first_cols), (over, far), dev(1 - LATT)),
    ]
    up_heat = [
        heat(5, (first_rows, mid), (under, mid), north),
        heat(6, (first_rows, last_cols), (under, near), dev(-1 + LATT)),
        heat(7, (first_rows, first_cols), (under, far), dev(-1 - LATT)),
    ]

    @pl.when(has_south)
    def _():
        for copy in down_heat:
            copy.start()

    @pl.when(has_north)
    def _():
        for copy in up_heat:
            copy.start()

    for copy in lon_heat:
        copy.start()

    to_east.wait_send()
    to_west.wait_send()

    @pl.when(has_south)
    def _():
        lax.fori_loop(0, blocks, lambda c, z: (lat_copy(0, c).wait_send(), z)[1], 0)

    @pl.when(has_north)
    def _():
        lax.fori_loop(0, blocks, lambda c, z: (lat_copy(1, c).wait_send(), z)[1], 0)

    for copy in lon_heat:
        copy.wait_recv()

    @pl.when(has_north)
    def _():
        for copy in down_heat:
            copy.wait_recv()

    @pl.when(has_south)
    def _():
        for copy in up_heat:
            copy.wait_recv()

    def peaks(i, carry):
        base = pl.multiple_of(i * CB, CB)
        h = hs[:, pl.ds(base, CB + 2 * LANES)]
        width = CB + 2 * LANES

        def ahead(v, k):
            return pltpu.roll(v, (width - k) % width, 1)

        m = jnp.maximum(h, ahead(h, 1))
        m = jnp.maximum(m, ahead(m, 2))
        sides = jnp.maximum(ahead(m, width - 4), ahead(m, 1))
        sides = sides[:, LANES : LANES + CB]
        center = h[:, LANES : LANES + CB]
        full = jnp.maximum(sides, center)
        height = full.shape[0]
        v = jnp.maximum(full, pltpu.roll(full, height - 1, 0))
        v = jnp.maximum(v, pltpu.roll(v, height - 2, 0))
        others = jnp.maximum(pltpu.roll(v, 4, 0), pltpu.roll(v, height - 1, 0))
        around = jnp.maximum(others, sides)
        margin_ref[0, :, pl.ds(base, CB)] = (center - around)[8 : 8 + rows]
        return carry

    lax.fori_loop(0, blocks, peaks, 0)

    for copy in lon_heat:
        copy.wait_send()

    @pl.when(has_south)
    def _():
        for copy in down_heat:
            copy.wait_send()

    @pl.when(has_north)
    def _():
        for copy in up_heat:
            copy.wait_send()


def solution(mesh):
    n = mesh.shape["lon"]

    def shards(features, conv_weight, conv_bias, head_weight, head_bias):
        _, rows, cols, chans = features.shape
        pairs = rows // 2
        blocks = cols // CB
        vmem = pl.BlockSpec(memory_space=pltpu.VMEM)
        return pl.pallas_call(
            lambda *refs: kernel(n, *refs),
            out_shape=(
                jax.ShapeDtypeStruct((1, rows, cols), jnp.float32),
                jax.ShapeDtypeStruct((1, 3, rows, cols), jnp.float32),
            ),
            in_specs=[
                pl.BlockSpec(memory_space=pl.ANY), vmem, vmem, vmem,
                pl.BlockSpec(memory_space=pltpu.SMEM),
            ],
            out_specs=(vmem, vmem),
            scratch_shapes=[
                pltpu.VMEM((rows, cols + 2 * PAD, chans), jnp.bfloat16),
                pltpu.VMEM((6 * LANES, 2 * LANES), jnp.bfloat16),
                pltpu.VMEM((4 * rows, pairs * LANES), jnp.bfloat16),
                pltpu.VMEM((2, cols, LANES), jnp.float32),
                pltpu.VMEM((CB, (pairs - 2) * LANES), jnp.bfloat16),
                pltpu.VMEM((4 * rows, cols), jnp.float32),
                pltpu.VMEM((2, cols // 2, LANES), jnp.bfloat16),
                pltpu.VMEM((2, cols // 2, LANES), jnp.bfloat16),
                pltpu.VMEM((rows + 16, cols + 2 * LANES), jnp.float32),
                pltpu.SemaphoreType.DMA((blocks,)),
                pltpu.SemaphoreType.DMA((2,)),
                pltpu.SemaphoreType.DMA((2,)),
                pltpu.SemaphoreType.DMA((2, blocks)),
                pltpu.SemaphoreType.DMA((2, blocks)),
                pltpu.SemaphoreType.DMA((8,)),
                pltpu.SemaphoreType.DMA((8,)),
            ],
            compiler_params=pltpu.CompilerParams(
                collective_id=0, has_side_effects=True, vmem_limit_bytes=56 * 1024 * 1024
            ),
            cost_estimate=pl.CostEstimate(
                flops=2 * rows * cols * chans * 9 * 64,
                bytes_accessed=2 * rows * cols * chans,
                transcendentals=rows * cols,
            ),
        )(features, conv_weight, conv_bias[None], head_weight, head_bias)

    in_specs = (P(("grp", "lon"), None, None, None), P(), P(), P(), P())
    out_specs = (P(("grp", "lon"), None, None), P(("grp", "lon"), None, None, None))
    return jax.shard_map(shards, mesh=mesh, in_specs=in_specs, out_specs=out_specs, check_vma=False)
```

```python
import jax
import jax.numpy as jnp
from jax import lax
from jax.experimental import pallas as pl
from jax.experimental.pallas import tpu as pltpu
from jax.sharding import PartitionSpec as P

LATT = 4
CB = 512
PAD = 16
LANES = 128
MESH = pl.DeviceIdType.MESH


def kernel(
    n, x_ref, cw_ref, cb_ref, hw_ref, hb_ref, margin_ref, regress_ref,
    xbuf, wbuf, hbig, pre_edge, hid, lg, sendbuf, recvbuf, hs,
    x_sem, rim_send, rim_recv, lat_send, lat_recv, heat_send, heat_recv,
):
    rows, cols = xbuf.shape[0], xbuf.shape[1] - 2 * PAD
    pairs = rows // 2
    blocks = cols // CB
    half = CB // 2
    t = lax.axis_index("lon")
    lat = lax.rem(t + 1, LATT)
    has_north = lat != 0
    has_south = lat != LATT - 1
    grp = lax.axis_index("grp")

    def dev(shift):
        return (grp, lax.rem(t + shift + n, n))

    north, south, west, east = dev(-1), dev(1), dev(-LATT), dev(LATT)

    def own_copy(c):
        start = pl.multiple_of(c * CB, CB)
        return pltpu.make_async_copy(
            x_ref.at[0, :, pl.ds(start, CB)],
            xbuf.at[:, pl.ds(PAD + start, CB)],
            x_sem.at[c],
        )

    for c in range(blocks):
        own_copy(c).start()

    barrier = pltpu.get_barrier_semaphore()

    def greet(target):
        pl.semaphore_signal(barrier, inc=1, device_id=target, device_id_type=MESH)

    greet(west)
    greet(east)

    @pl.when(has_north)
    def _():
        greet(north)
        greet(dev(-1 - LATT))
        greet(dev(-1 + LATT))

    @pl.when(has_south)
    def _():
        greet(south)
        greet(dev(1 - LATT))
        greet(dev(1 + LATT))

    zero_tap = jnp.zeros((64, LANES), jnp.bfloat16)

    def tap(a, b):
        return cw_ref[a, b] if 0 <= a <= 2 else zero_tap

    for b in range(3):
        for s in range(2):
            lo = (b * 2 + s) * LANES
            taps = [tap(s + 1, b), tap(s, b), tap(s - 1, b), tap(s + 2, b)]
            wbuf[lo : lo + LANES, :] = jnp.concatenate(taps, axis=0).T
    spread = (
        lax.broadcasted_iota(jnp.int32, (4 * rows, 4), 0) // rows
        == lax.broadcasted_iota(jnp.int32, (4 * rows, 4), 1)
    )
    spread = jnp.where(spread, 1.0, 0.0).astype(jnp.bfloat16)
    by_row = jnp.dot(spread, hw_ref[...], preferred_element_type=jnp.float32)
    wide = jnp.concatenate([by_row] * rows, axis=1)
    keep = (
        lax.rem(lax.broadcasted_iota(jnp.int32, wide.shape, 0), rows)
        == lax.broadcasted_iota(jnp.int32, wide.shape, 1) // 64
    )
    hbig[...] = jnp.where(keep, wide, 0.0).astype(jnp.bfloat16)

    @pl.when(jnp.logical_not(has_north))
    def _():
        recvbuf[0] = jnp.zeros(recvbuf.shape[1:], recvbuf.dtype)
        hs[0:8, :] = jnp.zeros((8, hs.shape[1]), hs.dtype)

    @pl.when(jnp.logical_not(has_south))
    def _():
        recvbuf[1] = jnp.zeros(recvbuf.shape[1:], recvbuf.dtype)
        hs[8 + rows : 16 + rows, :] = jnp.zeros((8, hs.shape[1]), hs.dtype)

    peers = 2 + jnp.where(has_north, 3, 0) + jnp.where(has_south, 3, 0)
    pl.semaphore_wait(barrier, peers)

    def remote(src, dst, send, recv, target):
        return pltpu.make_async_remote_copy(
            src_ref=src, dst_ref=dst, send_sem=send, recv_sem=recv,
            device_id=target, device_id_type=MESH,
        )

    to_east = remote(
        x_ref.at[0, :, pl.ds(cols - PAD, PAD)], xbuf.at[:, pl.ds(0, PAD)],
        rim_send.at[0], rim_recv.at[0], east,
    )
    to_west = remote(
        x_ref.at[0, :, pl.ds(0, PAD)], xbuf.at[:, pl.ds(cols + PAD, PAD)],
        rim_send.at[1], rim_recv.at[1], west,
    )
    to_east.start()
    to_west.start()

    low_lane = lax.broadcasted_iota(jnp.int32, (1, LANES), 1) < 64
    bias = jnp.concatenate([cb_ref[...], cb_ref[...]], axis=1)

    def lat_copy(way, c):
        part = pl.ds(pl.multiple_of(c * half, half), half)
        return remote(
            sendbuf.at[way, part], recvbuf.at[way, part],
            lat_send.at[way, c], lat_recv.at[way, c], south if way == 0 else north,
        )

    own_copy(0).wait()
    own_copy(1).wait()

    def first(i, carry):
        c = lax.rem(i + 1, blocks)
        base = pl.multiple_of(c * CB, CB)

        @pl.when(i + 2 < blocks)
        def _():
            own_copy(i + 2).wait()

        @pl.when(i == blocks - 2)
        def _():
            to_west.wait_recv()

        @pl.when(i == blocks - 1)
        def _():
            to_east.wait_recv()

        def products(p):
            win = jnp.concatenate(
                [xbuf[2 * p, pl.ds(base, CB + 2 * PAD)], xbuf[2 * p + 1, pl.ds(base, CB + 2 * PAD)]],
                axis=1,
            )
            taps = jnp.concatenate(
                [win[PAD - 1 + b : PAD - 1 + b + CB] for b in range(3)], axis=1
            )
            return jnp.dot(taps, wbuf[...], preferred_element_type=jnp.float32)

        def finish(p, main, above, below):
            pre = main + bias
            if p == 0:
                pre_edge[0, pl.ds(base, CB)] = pre + jnp.where(low_lane, 0.0, below)
            elif p == pairs - 1:
                pre_edge[1, pl.ds(base, CB)] = pre + jnp.where(low_lane, above, 0.0)
            else:
                pre = pre + jnp.where(low_lane, above, below)
                at = (p - 1) * LANES
                hid[:, at : at + LANES] = jnp.maximum(pre, 0.0).astype(jnp.bfloat16)

        before = None
        held = None
        for p in range(pairs):
            out = products(p)
            main, side = out[:, :LANES], out[:, LANES:]
            if p == 0:
                packed = jnp.where(low_lane, pltpu.roll(side[:half], 64, 1), side[half:])
                sendbuf[1, pl.ds(pl.multiple_of(c * half, half), half)] = packed.astype(jnp.bfloat16)
            else:
                finish(p - 1, held[0], before, side)
                before = held[1]
            held = (main, side)
        packed = jnp.where(low_lane, held[1][:half], pltpu.roll(held[1][half:], 64, 1))
        sendbuf[0, pl.ds(pl.multiple_of(c * half, half), half)] = packed.astype(jnp.bfloat16)
        finish(pairs - 1, held[0], before, None)

        @pl.when(has_south)
        def _():
            lat_copy(0, c).start()

        @pl.when(has_north)
        def _():
            lat_copy(1, c).start()

        lg[:, pl.ds(base, CB)] = lax.dot_general(
            hbig[:, LANES : (pairs - 1) * LANES], hid[...],
            (((1,), (1,)), ((), ())), preferred_element_type=jnp.float32,
        )
        return carry

    lax.fori_loop(0, blocks, first, 0)

    def second(i, carry):
        c = lax.rem(i + 1, blocks)
        base = pl.multiple_of(c * CB, CB)
        part = pl.ds(pl.multiple_of(c * half, half), half)

        @pl.when(has_north)
        def _():
            lat_copy(0, c).wait_recv()

        @pl.when(has_south)
        def _():
            lat_copy(1, c).wait_recv()

        above = recvbuf[0, part].astype(jnp.float32)
        above = jnp.concatenate([above, pltpu.roll(above, 64, 1)], axis=0)
        below = recvbuf[1, part].astype(jnp.float32)
        below = jnp.concatenate([pltpu.roll(below, 64, 1), below], axis=0)
        top = pre_edge[0, pl.ds(base, CB)] + jnp.where(low_lane, above, 0.0)
        bottom = pre_edge[1, pl.ds(base, CB)] + jnp.where(low_lane, 0.0, below)
        edge = jnp.maximum(jnp.concatenate([top, bottom], axis=1), 0.0).astype(jnp.bfloat16)
        heads = jnp.concatenate([hbig[:, :LANES], hbig[:, (pairs - 1) * LANES :]], axis=1)
        logits = lg[:, pl.ds(base, CB)] + lax.dot_general(
            heads, edge, (((1,), (1,)), ((), ())), preferred_element_type=jnp.float32
        )
        hs[8 : 8 + rows, pl.ds(LANES + base, CB)] = jax.nn.sigmoid(logits[:rows] + hb_ref[0])
        for k in range(1, 4):
            regress_ref[0, k - 1, :, pl.ds(base, CB)] = (
                logits[k * rows : (k + 1) * rows] + hb_ref[k]
            )
        return carry

    lax.fori_loop(0, blocks, second, 0)

    own, far = pl.ds(8, rows), pl.ds(LANES + cols, LANES)
    first_cols, last_cols = pl.ds(LANES, LANES), pl.ds(cols, LANES)
    near = pl.ds(0, LANES)
    mid = pl.ds(LANES, cols)
    first_rows, last_rows = pl.ds(8, 8), pl.ds(rows, 8)
    over, under = pl.ds(0, 8), pl.ds(8 + rows, 8)

    def heat(k, src, dst, target):
        return remote(hs.at[src], hs.at[dst], heat_send.at[k], heat_recv.at[k], target)

    lon_heat = [
        heat(0, (own, last_cols), (own, near), east),
        heat(1, (own, first_cols), (own, far), west),
    ]
    down_heat = [
        heat(2, (last_rows, mid), (over, mid), south),
        heat(3, (last_rows, last_cols), (over, near), dev(1 + LATT)),
        heat(4, (last_rows, first_cols), (over, far), dev(1 - LATT)),
    ]
    up_heat = [
        heat(5, (first_rows, mid), (under, mid), north),
        heat(6, (first_rows, last_cols), (under, near), dev(-1 + LATT)),
        heat(7, (first_rows, first_cols), (under, far), dev(-1 - LATT)),
    ]

    @pl.when(has_south)
    def _():
        for copy in down_heat:
            copy.start()

    @pl.when(has_north)
    def _():
        for copy in up_heat:
            copy.start()

    for copy in lon_heat:
        copy.start()

    to_east.wait_send()
    to_west.wait_send()

    @pl.when(has_south)
    def _():
        lax.fori_loop(0, blocks, lambda c, z: (lat_copy(0, c).wait_send(), z)[1], 0)

    @pl.when(has_north)
    def _():
        lax.fori_loop(0, blocks, lambda c, z: (lat_copy(1, c).wait_send(), z)[1], 0)

    for copy in lon_heat:
        copy.wait_recv()

    @pl.when(has_north)
    def _():
        for copy in down_heat:
            copy.wait_recv()

    @pl.when(has_south)
    def _():
        for copy in up_heat:
            copy.wait_recv()

    def peaks(i, carry):
        base = pl.multiple_of(i * CB, CB)
        h = hs[:, pl.ds(base, CB + 2 * LANES)]
        width = CB + 2 * LANES

        def ahead(v, k):
            return pltpu.roll(v, (width - k) % width, 1)

        m = jnp.maximum(h, ahead(h, 1))
        m = jnp.maximum(m, ahead(m, 2))
        sides = jnp.maximum(ahead(m, width - 4), ahead(m, 1))
        sides = sides[:, LANES : LANES + CB]
        center = h[:, LANES : LANES + CB]
        full = jnp.maximum(sides, center)
        height = full.shape[0]
        v = jnp.maximum(full, pltpu.roll(full, height - 1, 0))
        v = jnp.maximum(v, pltpu.roll(v, height - 2, 0))
        others = jnp.maximum(pltpu.roll(v, 4, 0), pltpu.roll(v, height - 1, 0))
        around = jnp.maximum(others, sides)
        margin_ref[0, :, pl.ds(base, CB)] = (center - around)[8 : 8 + rows]
        return carry

    lax.fori_loop(0, blocks, peaks, 0)

    for copy in lon_heat:
        copy.wait_send()

    @pl.when(has_south)
    def _():
        for copy in down_heat:
            copy.wait_send()

    @pl.when(has_north)
    def _():
        for copy in up_heat:
            copy.wait_send()


def solution(mesh):
    n = mesh.shape["lon"]

    def shards(features, conv_weight, conv_bias, head_weight, head_bias):
        _, rows, cols, chans = features.shape
        pairs = rows // 2
        blocks = cols // CB
        vmem = pl.BlockSpec(memory_space=pltpu.VMEM)
        return pl.pallas_call(
            lambda *refs: kernel(n, *refs),
            out_shape=(
                jax.ShapeDtypeStruct((1, rows, cols), jnp.float32),
                jax.ShapeDtypeStruct((1, 3, rows, cols), jnp.float32),
            ),
            in_specs=[
                pl.BlockSpec(memory_space=pl.ANY), vmem, vmem, vmem,
                pl.BlockSpec(memory_space=pltpu.SMEM),
            ],
            out_specs=(vmem, vmem),
            scratch_shapes=[
                pltpu.VMEM((rows, cols + 2 * PAD, chans), jnp.bfloat16),
                pltpu.VMEM((6 * LANES, 2 * LANES), jnp.bfloat16),
                pltpu.VMEM((4 * rows, pairs * LANES), jnp.bfloat16),
                pltpu.VMEM((2, cols, LANES), jnp.float32),
                pltpu.VMEM((CB, (pairs - 2) * LANES), jnp.bfloat16),
                pltpu.VMEM((4 * rows, cols), jnp.float32),
                pltpu.VMEM((2, cols // 2, LANES), jnp.bfloat16),
                pltpu.VMEM((2, cols // 2, LANES), jnp.bfloat16),
                pltpu.VMEM((rows + 16, cols + 2 * LANES), jnp.float32),
                pltpu.SemaphoreType.DMA((blocks,)),
                pltpu.SemaphoreType.DMA((2,)),
                pltpu.SemaphoreType.DMA((2,)),
                pltpu.SemaphoreType.DMA((2, blocks)),
                pltpu.SemaphoreType.DMA((2, blocks)),
                pltpu.SemaphoreType.DMA((8,)),
                pltpu.SemaphoreType.DMA((8,)),
            ],
            compiler_params=pltpu.CompilerParams(
                collective_id=0, has_side_effects=True, vmem_limit_bytes=56 * 1024 * 1024
            ),
            cost_estimate=pl.CostEstimate(
                flops=2 * rows * cols * chans * 9 * 64,
                bytes_accessed=2 * rows * cols * chans,
                transcendentals=rows * cols,
            ),
        )(features, jnp.swapaxes(conv_weight, 2, 3), conv_bias[None], head_weight.T, head_bias)

    in_specs = (P(("grp", "lon"), None, None, None), P(), P(), P(), P())
    out_specs = (P(("grp", "lon"), None, None), P(("grp", "lon"), None, None, None))
    return jax.shard_map(shards, mesh=mesh, in_specs=in_specs, out_specs=out_specs, check_vma=False)
```

```python
import jax
import jax.numpy as jnp
from jax import lax
from jax.experimental import pallas as pl
from jax.experimental.pallas import tpu as pltpu
from jax.sharding import PartitionSpec as P

LATT = 4
CB = 512
PAD = 16
LANES = 128
MESH = pl.DeviceIdType.MESH


def kernel(
    n, x_ref, cw_ref, cb_ref, hw_ref, hb_ref, margin_ref, regress_ref,
    xbuf, wbuf, hbig, pre_edge, hid, lg, sendbuf, recvbuf, hs,
    x_sem, rim_send, rim_recv, lat_send, lat_recv, heat_send, heat_recv,
):
    rows, cols = xbuf.shape[0], xbuf.shape[1] - 2 * PAD
    pairs = rows // 2
    blocks = cols // CB
    half = CB // 2
    t = lax.axis_index("lon")
    lat = lax.rem(t + 1, LATT)
    has_north = lat != 0
    has_south = lat != LATT - 1
    grp = lax.axis_index("grp")

    def dev(shift):
        return (grp, lax.rem(t + shift + n, n))

    north, south, west, east = dev(-1), dev(1), dev(-LATT), dev(LATT)

    def own_copy(c):
        start = pl.multiple_of(c * CB, CB)
        return pltpu.make_async_copy(
            x_ref.at[0, :, pl.ds(start, CB)],
            xbuf.at[:, pl.ds(PAD + start, CB)],
            x_sem.at[c],
        )

    for c in range(blocks):
        own_copy(c).start()

    barrier = pltpu.get_barrier_semaphore()

    def greet(target):
        pl.semaphore_signal(barrier, inc=1, device_id=target, device_id_type=MESH)

    greet(west)
    greet(east)

    @pl.when(has_north)
    def _():
        greet(north)
        greet(dev(-1 - LATT))
        greet(dev(-1 + LATT))

    @pl.when(has_south)
    def _():
        greet(south)
        greet(dev(1 - LATT))
        greet(dev(1 + LATT))

    zero_tap = jnp.zeros((64, LANES), jnp.bfloat16)

    def tap(a, b):
        return cw_ref[a, b] if 0 <= a <= 2 else zero_tap

    for b in range(3):
        for s in range(2):
            lo = (b * 2 + s) * LANES
            taps = [tap(s + 1, b), tap(s, b), tap(s - 1, b), tap(s + 2, b)]
            wbuf[lo : lo + LANES, :] = jnp.concatenate(taps, axis=0).T
    spread = (
        lax.broadcasted_iota(jnp.int32, (4 * rows, 4), 0) // rows
        == lax.broadcasted_iota(jnp.int32, (4 * rows, 4), 1)
    )
    spread = jnp.where(spread, 1.0, 0.0).astype(jnp.bfloat16)
    by_row = jnp.dot(spread, hw_ref[...], preferred_element_type=jnp.float32)
    wide = jnp.concatenate([by_row] * rows, axis=1)
    keep = (
        lax.rem(lax.broadcasted_iota(jnp.int32, wide.shape, 0), rows)
        == lax.broadcasted_iota(jnp.int32, wide.shape, 1) // 64
    )
    hbig[...] = jnp.where(keep, wide, 0.0).astype(jnp.bfloat16)

    @pl.when(jnp.logical_not(has_north))
    def _():
        recvbuf[0] = jnp.zeros(recvbuf.shape[1:], recvbuf.dtype)
        hs[0:8, :] = jnp.zeros((8, hs.shape[1]), hs.dtype)

    @pl.when(jnp.logical_not(has_south))
    def _():
        recvbuf[1] = jnp.zeros(recvbuf.shape[1:], recvbuf.dtype)
        hs[8 + rows : 16 + rows, :] = jnp.zeros((8, hs.shape[1]), hs.dtype)

    peers = 2 + jnp.where(has_north, 3, 0) + jnp.where(has_south, 3, 0)
    pl.semaphore_wait(barrier, peers)

    def remote(src, dst, send, recv, target):
        return pltpu.make_async_remote_copy(
            src_ref=src, dst_ref=dst, send_sem=send, recv_sem=recv,
            device_id=target, device_id_type=MESH,
        )

    to_east = remote(
        x_ref.at[0, :, pl.ds(cols - PAD, PAD)], xbuf.at[:, pl.ds(0, PAD)],
        rim_send.at[0], rim_recv.at[0], east,
    )
    to_west = remote(
        x_ref.at[0, :, pl.ds(0, PAD)], xbuf.at[:, pl.ds(cols + PAD, PAD)],
        rim_send.at[1], rim_recv.at[1], west,
    )
    to_east.start()
    to_west.start()

    low_lane = lax.broadcasted_iota(jnp.int32, (1, LANES), 1) < 64
    bias = jnp.concatenate([cb_ref[...], cb_ref[...]], axis=1)

    def lat_copy(way, c):
        part = pl.ds(pl.multiple_of(c * half, half), half)
        return remote(
            sendbuf.at[way, part], recvbuf.at[way, part],
            lat_send.at[way, c], lat_recv.at[way, c], south if way == 0 else north,
        )

    own_copy(0).wait()
    own_copy(1).wait()

    def first(i, carry):
        c = lax.rem(i + 1, blocks)
        base = pl.multiple_of(c * CB, CB)

        @pl.when(i + 2 < blocks)
        def _():
            own_copy(i + 2).wait()

        @pl.when(i == blocks - 2)
        def _():
            to_west.wait_recv()

        @pl.when(i == blocks - 1)
        def _():
            to_east.wait_recv()

        def products(p):
            win = jnp.concatenate(
                [xbuf[2 * p, pl.ds(base, CB + 2 * PAD)], xbuf[2 * p + 1, pl.ds(base, CB + 2 * PAD)]],
                axis=1,
            )
            taps = jnp.concatenate(
                [win[PAD - 1 + b : PAD - 1 + b + CB] for b in range(3)], axis=1
            )
            return jnp.dot(taps, wbuf[...], preferred_element_type=jnp.float32)

        def finish(p, main, above, below):
            pre = main + bias
            if p == 0:
                pre_edge[0, pl.ds(base, CB)] = pre + jnp.where(low_lane, 0.0, below)
            elif p == pairs - 1:
                pre_edge[1, pl.ds(base, CB)] = pre + jnp.where(low_lane, above, 0.0)
            else:
                pre = pre + jnp.where(low_lane, above, below)
                at = (p - 1) * LANES
                hid[:, at : at + LANES] = jnp.maximum(pre, 0.0).astype(jnp.bfloat16)

        before = None
        held = None
        for p in range(pairs):
            out = products(p)
            main, side = out[:, :LANES], out[:, LANES:]
            if p == 0:
                packed = jnp.where(low_lane, pltpu.roll(side[:half], 64, 1), side[half:])
                sendbuf[1, pl.ds(pl.multiple_of(c * half, half), half)] = packed.astype(jnp.bfloat16)
            else:
                finish(p - 1, held[0], before, side)
                before = held[1]
            held = (main, side)
        packed = jnp.where(low_lane, held[1][:half], pltpu.roll(held[1][half:], 64, 1))
        sendbuf[0, pl.ds(pl.multiple_of(c * half, half), half)] = packed.astype(jnp.bfloat16)
        finish(pairs - 1, held[0], before, None)

        @pl.when(has_south)
        def _():
            lat_copy(0, c).start()

        @pl.when(has_north)
        def _():
            lat_copy(1, c).start()

        lg[:, pl.ds(base, CB)] = lax.dot_general(
            hbig[:, LANES : (pairs - 1) * LANES], hid[...],
            (((1,), (1,)), ((), ())), preferred_element_type=jnp.float32,
        )
        return carry

    lax.fori_loop(0, blocks, first, 0)

    def second(i, carry):
        c = lax.rem(i + 1, blocks)
        base = pl.multiple_of(c * CB, CB)
        part = pl.ds(pl.multiple_of(c * half, half), half)

        @pl.when(has_north)
        def _():
            lat_copy(0, c).wait_recv()

        @pl.when(has_south)
        def _():
            lat_copy(1, c).wait_recv()

        above = recvbuf[0, part].astype(jnp.float32)
        above = jnp.concatenate([above, pltpu.roll(above, 64, 1)], axis=0)
        below = recvbuf[1, part].astype(jnp.float32)
        below = jnp.concatenate([pltpu.roll(below, 64, 1), below], axis=0)
        top = pre_edge[0, pl.ds(base, CB)] + jnp.where(low_lane, above, 0.0)
        bottom = pre_edge[1, pl.ds(base, CB)] + jnp.where(low_lane, 0.0, below)
        edge = jnp.maximum(jnp.concatenate([top, bottom], axis=1), 0.0).astype(jnp.bfloat16)
        heads = jnp.concatenate([hbig[:, :LANES], hbig[:, (pairs - 1) * LANES :]], axis=1)
        logits = lg[:, pl.ds(base, CB)] + lax.dot_general(
            heads, edge, (((1,), (1,)), ((), ())), preferred_element_type=jnp.float32
        )
        hs[8 : 8 + rows, pl.ds(LANES + base, CB)] = jax.nn.sigmoid(logits[:rows] + hb_ref[0])
        for k in range(1, 4):
            regress_ref[0, k - 1, :, pl.ds(base, CB)] = logits[k * rows : (k + 1) * rows]
        return carry

    lax.fori_loop(0, blocks, second, 0)

    own, far = pl.ds(8, rows), pl.ds(LANES + cols, LANES)
    first_cols, last_cols = pl.ds(LANES, LANES), pl.ds(cols, LANES)
    near = pl.ds(0, LANES)
    mid = pl.ds(LANES, cols)
    first_rows, last_rows = pl.ds(8, 8), pl.ds(rows, 8)
    over, under = pl.ds(0, 8), pl.ds(8 + rows, 8)

    def heat(k, src, dst, target):
        return remote(hs.at[src], hs.at[dst], heat_send.at[k], heat_recv.at[k], target)

    lon_heat = [
        heat(0, (own, last_cols), (own, near), east),
        heat(1, (own, first_cols), (own, far), west),
    ]
    down_heat = [
        heat(2, (last_rows, mid), (over, mid), south),
        heat(3, (last_rows, last_cols), (over, near), dev(1 + LATT)),
        heat(4, (last_rows, first_cols), (over, far), dev(1 - LATT)),
    ]
    up_heat = [
        heat(5, (first_rows, mid), (under, mid), north),
        heat(6, (first_rows, last_cols), (under, near), dev(-1 + LATT)),
        heat(7, (first_rows, first_cols), (under, far), dev(-1 - LATT)),
    ]

    @pl.when(has_south)
    def _():
        for copy in down_heat:
            copy.start()

    @pl.when(has_north)
    def _():
        for copy in up_heat:
            copy.start()

    for copy in lon_heat:
        copy.start()

    to_east.wait_send()
    to_west.wait_send()

    @pl.when(has_south)
    def _():
        lax.fori_loop(0, blocks, lambda c, z: (lat_copy(0, c).wait_send(), z)[1], 0)

    @pl.when(has_north)
    def _():
        lax.fori_loop(0, blocks, lambda c, z: (lat_copy(1, c).wait_send(), z)[1], 0)

    for copy in lon_heat:
        copy.wait_recv()

    @pl.when(has_north)
    def _():
        for copy in down_heat:
            copy.wait_recv()

    @pl.when(has_south)
    def _():
        for copy in up_heat:
            copy.wait_recv()

    def peaks(i, carry):
        base = pl.multiple_of(i * CB, CB)
        h = hs[:, pl.ds(base, CB + 2 * LANES)]
        width = CB + 2 * LANES

        def ahead(v, k):
            return pltpu.roll(v, (width - k) % width, 1)

        m = jnp.maximum(h, ahead(h, 1))
        m = jnp.maximum(m, ahead(m, 2))
        sides = jnp.maximum(ahead(m, width - 4), ahead(m, 1))
        sides = sides[:, LANES : LANES + CB]
        center = h[:, LANES : LANES + CB]
        full = jnp.maximum(sides, center)
        height = full.shape[0]
        v = jnp.maximum(full, pltpu.roll(full, height - 1, 0))
        v = jnp.maximum(v, pltpu.roll(v, height - 2, 0))
        others = jnp.maximum(pltpu.roll(v, 4, 0), pltpu.roll(v, height - 1, 0))
        around = jnp.maximum(others, sides)
        margin_ref[0, :, pl.ds(base, CB)] = (center - around)[8 : 8 + rows]
        return carry

    lax.fori_loop(0, blocks, peaks, 0)

    for copy in lon_heat:
        copy.wait_send()

    @pl.when(has_south)
    def _():
        for copy in down_heat:
            copy.wait_send()

    @pl.when(has_north)
    def _():
        for copy in up_heat:
            copy.wait_send()


def deliver(margin_in, raw_in, hb_ref, margin_out, regress_out):
    margin_out[...] = margin_in[...]
    for k in range(1, 4):
        regress_out[0, k - 1] = raw_in[0, k - 1] + hb_ref[k]


def solution(mesh):
    n = mesh.shape["lon"]

    def shards(features, conv_weight, conv_bias, head_weight, head_bias):
        _, rows, cols, chans = features.shape
        pairs = rows // 2
        blocks = cols // CB
        vmem = pl.BlockSpec(memory_space=pltpu.VMEM)
        margin, raw = pl.pallas_call(
            lambda *refs: kernel(n, *refs),
            out_shape=(
                jax.ShapeDtypeStruct((1, rows, cols), jnp.float32),
                jax.ShapeDtypeStruct((1, 3, rows, cols), jnp.float32),
            ),
            in_specs=[
                pl.BlockSpec(memory_space=pl.ANY), vmem, vmem, vmem,
                pl.BlockSpec(memory_space=pltpu.SMEM),
            ],
            out_specs=(vmem, vmem),
            scratch_shapes=[
                pltpu.VMEM((rows, cols + 2 * PAD, chans), jnp.bfloat16),
                pltpu.VMEM((6 * LANES, 2 * LANES), jnp.bfloat16),
                pltpu.VMEM((4 * rows, pairs * LANES), jnp.bfloat16),
                pltpu.VMEM((2, cols, LANES), jnp.float32),
                pltpu.VMEM((CB, (pairs - 2) * LANES), jnp.bfloat16),
                pltpu.VMEM((4 * rows, cols), jnp.float32),
                pltpu.VMEM((2, cols // 2, LANES), jnp.bfloat16),
                pltpu.VMEM((2, cols // 2, LANES), jnp.bfloat16),
                pltpu.VMEM((rows + 16, cols + 2 * LANES), jnp.float32),
                pltpu.SemaphoreType.DMA((blocks,)),
                pltpu.SemaphoreType.DMA((2,)),
                pltpu.SemaphoreType.DMA((2,)),
                pltpu.SemaphoreType.DMA((2, blocks)),
                pltpu.SemaphoreType.DMA((2, blocks)),
                pltpu.SemaphoreType.DMA((8,)),
                pltpu.SemaphoreType.DMA((8,)),
            ],
            compiler_params=pltpu.CompilerParams(
                collective_id=0, has_side_effects=True, vmem_limit_bytes=56 * 1024 * 1024
            ),
            cost_estimate=pl.CostEstimate(
                flops=2 * rows * cols * chans * 9 * 64,
                bytes_accessed=2 * rows * cols * chans,
                transcendentals=rows * cols,
            ),
        )(features, jnp.swapaxes(conv_weight, 2, 3), conv_bias[None], head_weight.T, head_bias)
        span = cols // 2
        margin_spec = pl.BlockSpec((1, rows, span), lambda i: (0, 0, i))
        regress_spec = pl.BlockSpec((1, 3, rows, span), lambda i: (0, 0, 0, i))
        return pl.pallas_call(
            deliver,
            grid=(2,),
            out_shape=(
                jax.ShapeDtypeStruct(margin.shape, jnp.float32),
                jax.ShapeDtypeStruct(raw.shape, jnp.float32),
            ),
            in_specs=[margin_spec, regress_spec, pl.BlockSpec(memory_space=pltpu.SMEM)],
            out_specs=(margin_spec, regress_spec),
        )(margin, raw, head_bias)

    in_specs = (P(("grp", "lon"), None, None, None), P(), P(), P(), P())
    out_specs = (P(("grp", "lon"), None, None), P(("grp", "lon"), None, None, None))
    return jax.shard_map(shards, mesh=mesh, in_specs=in_specs, out_specs=out_specs, check_vma=False)
```
